32 devices in a mesh: dp: 2 (over core), seq: 16 (over z, y, x).
Axes of the slice: x: 2, y: 2, z: 4, core: 2. Of those that a mesh axis runs over, the one named last changes fastest.
Arguments:
- mapped_askers: bfloat16 [2, 4096, 1024], P('dp', 'seq'), may hold values from -6 to 6
- mapped_lookups: bfloat16 [2, 4096, 1024], P('dp', 'seq'), may hold values from -6 to 6
- mapped_contents: bfloat16 [2, 4096, 1024], P('dp', 'seq'), may hold values from -24 to 24
- result_cotangent: bfloat16 [2, 4096, 1024], P('dp', 'seq'), may hold values from -6 to 6
- result_weight_matrix: bfloat16 [1024, 1024], replicated, may hold values from -0.1875 to 0.1875
- reference_comb_shift: int32 [16, 32], P('seq'), may hold values from 0 to 7
- symbol_frame_label: int32 [4096], replicated, may hold values from 0 to 7, never falling along the last dimension, each value on 1 to 1024 neighbouring positions
Outputs:
- sublayer_out: bfloat16 [2, 4096, 1024], P('dp', 'seq')
- query_grad: bfloat16 [2, 4096, 1024], P('dp', 'seq')
- key_grad: bfloat16 [2, 4096, 1024], P('dp', 'seq')
- value_grad: bfloat16 [2, 4096, 1024], P('dp', 'seq')
- weight_grad: float32 [1024, 1024], P(('dp', 'seq'))
The draws below stay inside these ranges and needn't reach their ends.
All inputs are finite; a program needn't handle non-finite values.
Results may differ from the reference program's by a relative error of at most 0.012.
Values may be sent and summed in bfloat16 or wider, within the bound.
A program may use at most 128 MiB of HBM per device.

```python
import math
import jax
import jax.numpy as jnp
import numpy as np
from jax import lax

D = 1024
HEADS = 8
HALF_SPAN = 256
FRAME_SHARDS = 8
PIECE_SYMBOLS = 256
PIL_SHARD = 32
FRAME_PILOTS = 256
ROUND_SYMBOLS = 4096
FRAMES = 2
PASSES = 2
FRAME_NUMBER = 8
N_SEQ = 16


def paired(key):
    full_shape = (PASSES, ROUND_SYMBOLS, D)
    query_key = jax.random.fold_in(key, 101)
    keys_key = jax.random.fold_in(key, 102)
    mapped_askers = jnp.clip(1.1 * jax.random.normal(query_key, full_shape, jnp.float32), -6.0, 6.0)
    keyset = jnp.clip(1.1 * jax.random.normal(keys_key, full_shape, jnp.float32), -6.0, 6.0)
    return (mapped_askers, keyset)


def draw_mapped_askers(key, part):
    return paired(key)[0].astype(jnp.bfloat16)


def draw_mapped_lookups(key, part):
    return paired(key)[1].astype(jnp.bfloat16)


def place_ends(values, own_key, low, top_value):
    place = [jax.random.randint(jax.random.fold_in(own_key, axis), (), 0, length) for axis, length in enumerate(values.shape)]
    main_axis = values.shape.index(max(values.shape))
    beside = place[:main_axis] + [(place[main_axis] + 1) % values.shape[main_axis]] + place[main_axis + 1:]
    return values.at[tuple(place)].set(low).at[tuple(beside)].set(top_value)


def shard_levels(key, dims, shards, smallest, high):
    def one(dim, shards_of):
        draws = jax.random.uniform(jax.random.fold_in(jax.random.fold_in(key, 6), dim), (shards_of,), jnp.float32, smallest / len(shards), high / len(shards))
        return jnp.repeat(jnp.exp(draws), dims[dim] // shards_of).reshape((-1,) + (1,) * (len(dims) - dim - 1))

    factor_of = one(*shards[0])
    for cut in shards[1:]:
        factor_of = factor_of * one(*cut)
    return factor_of


def profile(count, total, most, slope):
    portions = [(1 << 20) // math.isqrt(grade ** slope) + 1 for grade in range(2, count + 1)]
    spare, holding = total - most - (count - 1), [1] * (count - 1)
    while spare > 0:
        free = [i for i in range(count - 1) if holding[i] < most]
        pool, budget = sum([portions[i] for i in free]), spare
        for i in free:
            more = min(most - holding[i], max(1, budget * portions[i] // pool), spare)
            holding[i] = holding[i] + more
            spare = spare - more
    return np.array([most] + holding)


def ragged(rng, number_of, total, reach, slope):
    if number_of == 2:
        one = jax.random.randint(rng, (), max(1, total - reach), min(reach, total - 1) + 1)
        return jnp.stack([one, total - one])
    tallies = jnp.asarray(profile(number_of, total, reach, slope), jnp.int32)
    couples = (number_of - 1) // 2
    source_of, taker = tallies[1:1 + 2 * couples:2], tallies[2:2 + 2 * couples:2]
    room = jnp.minimum(source_of - 1, reach - taker)
    moved = jax.random.randint(jax.random.fold_in(rng, 1), (couples,), 0, 1 << 20) % (room + 1)
    tallies = tallies.at[1:1 + 2 * couples:2].set(source_of - moved).at[2:2 + 2 * couples:2].set(taker + moved)
    return tallies[jax.random.permutation(jax.random.fold_in(rng, 2), number_of)]


def bell_draw(stream_key, dims, width, reach, shards=(), kind=jnp.bfloat16):
    level = shard_levels(stream_key, dims, shards, -0.22, 0.18) if shards else 1.0
    entries = jax.random.normal(stream_key, dims, jnp.float32) * width * level
    return jnp.minimum(jnp.maximum(entries, -reach), reach).astype(kind)


def setup_inputs(seed: int = 0) -> dict:
    streams_of = jax.random.split(jax.random.key(seed), 8)
    mapped_askers = draw_mapped_askers(jax.random.fold_in(streams_of[7], 71), 0)
    mapped_lookups = draw_mapped_lookups(jax.random.fold_in(streams_of[7], 71), 0)
    mapped_contents = bell_draw(streams_of[2], (PASSES, ROUND_SYMBOLS, D), 4.0, 24.0, ((0, 2), (1, 16)))
    result_cotangent = bell_draw(streams_of[3], (PASSES, ROUND_SYMBOLS, D), 1.0, 6.0, ((0, 2), (1, 16)))
    result_weight_matrix = bell_draw(streams_of[4], (D, D), D ** -0.5, 0.1875)
    reference_comb_shift = place_ends(jax.random.randint(streams_of[5], (N_SEQ, PIL_SHARD), 0, PIECE_SYMBOLS // PIL_SHARD), jax.random.fold_in(streams_of[5], 1), 0, (PIECE_SYMBOLS // PIL_SHARD) - 1).astype(jnp.int32)
    symbol_frame_label = jnp.searchsorted(jnp.cumsum(ragged(streams_of[6], FRAME_NUMBER, ROUND_SYMBOLS, 4 * PIECE_SYMBOLS, 1)), jnp.arange(ROUND_SYMBOLS), side="right").astype(jnp.int32)
    return dict(mapped_askers=mapped_askers, mapped_lookups=mapped_lookups, mapped_contents=mapped_contents, result_cotangent=result_cotangent, result_weight_matrix=result_weight_matrix, reference_comb_shift=reference_comb_shift, symbol_frame_label=symbol_frame_label)


def joint_admit_filter(neighbor_frame_label, overall_line_number):
    query_rows = jnp.arange(overall_line_number)[:, None] + HALF_SPAN
    key_cols = jnp.arange(overall_line_number + 2 * HALF_SPAN)[None, :]
    inside_local_distance = jnp.abs(query_rows - key_cols) <= HALF_SPAN
    asker_frame_label = neighbor_frame_label[HALF_SPAN:HALF_SPAN + overall_line_number]
    same_frame_filter = asker_frame_label[:, None] == neighbor_frame_label[None, :]
    return inside_local_distance & same_frame_filter

def attend_shard(query_block, key_win, val_win, key_pil, val_pil, local_admit_filter, grad_att):
    head_dim = query_block.shape[1] // HEADS
    scaling = 1.0 / math.sqrt(head_dim)

    def split_heads(matrix):
        return jnp.transpose(matrix.reshape(matrix.shape[0], HEADS, head_dim), (1, 0, 2))

    def join_heads(matrix):
        return jnp.transpose(matrix, (1, 0, 2)).reshape(matrix.shape[1], HEADS * head_dim)

    def one_head(round_arguments):
        query_head, key_head, val_head, pilot_key, pilot_val, grad_head = round_arguments
        score_win = jnp.dot(query_head, key_head.T, preferred_element_type=jnp.float32) * scaling
        score_win = jnp.where(local_admit_filter, score_win, -jnp.inf)
        score_pil = jnp.dot(query_head, pilot_key.T, preferred_element_type=jnp.float32) * scaling
        row_max = jnp.maximum(lax.optimization_barrier(jnp.max(score_win, axis=1)), lax.optimization_barrier(jnp.max(score_pil, axis=1)))[:, None]
        exp_win = jnp.exp(score_win - row_max)
        exp_pil = jnp.exp(score_pil - row_max)
        softmax_total = lax.optimization_barrier(jnp.sum(exp_win, axis=1, keepdims=True)) + lax.optimization_barrier(jnp.sum(exp_pil, axis=1, keepdims=True))
        prob_win = exp_win / softmax_total
        prob_pil = exp_pil / softmax_total
        weight_win = prob_win.astype(jnp.bfloat16)
        weight_pil = prob_pil.astype(jnp.bfloat16)
        attended = (jnp.dot(weight_win, val_head, preferred_element_type=jnp.float32) + jnp.dot(weight_pil, pilot_val, preferred_element_type=jnp.float32)).astype(jnp.bfloat16)
        dprob_win = jnp.dot(grad_head, val_head.T, preferred_element_type=jnp.float32)
        dprob_pil = jnp.dot(grad_head, pilot_val.T, preferred_element_type=jnp.float32)
        delta = lax.optimization_barrier(jnp.sum(grad_head.astype(jnp.float32) * attended.astype(jnp.float32), axis=1, keepdims=True))
        dscore_win = (prob_win * (dprob_win - delta)).astype(jnp.bfloat16)
        dscore_pil = (prob_pil * (dprob_pil - delta)).astype(jnp.bfloat16)
        query_grad = (jnp.dot(dscore_win, key_head, preferred_element_type=jnp.float32) + jnp.dot(dscore_pil, pilot_key, preferred_element_type=jnp.float32)) * scaling
        keywin_grad = jnp.dot(dscore_win.T, query_head, preferred_element_type=jnp.float32) * scaling
        valwin_grad = jnp.dot(weight_win.T, grad_head, preferred_element_type=jnp.float32)
        keypil_grad = jnp.dot(dscore_pil.T, query_head, preferred_element_type=jnp.float32) * scaling
        valpil_grad = jnp.dot(weight_pil.T, grad_head, preferred_element_type=jnp.float32)
        return (attended, query_grad, keywin_grad, valwin_grad, keypil_grad, valpil_grad)
    stacked = lax.map(one_head, (split_heads(query_block), split_heads(key_win), split_heads(val_win), split_heads(key_pil), split_heads(val_pil), split_heads(grad_att)))
    return tuple((join_heads(matrix) for matrix in stacked))

def round_iteration(asker_per_round, lookup_per_round, content_per_round, derivative_per_round, result_weight_matrix, reference_comb_shift, symbol_frame_label):
    grad_att = jnp.dot(derivative_per_round, result_weight_matrix.T, preferred_element_type=jnp.float32).astype(jnp.bfloat16)
    slot_width = PIECE_SYMBOLS // PIL_SHARD
    positions = (jnp.arange(N_SEQ, dtype=jnp.int32)[:, None] * PIECE_SYMBOLS + jnp.arange(PIL_SHARD, dtype=jnp.int32)[None, :] * slot_width + reference_comb_shift).astype(jnp.int32)
    frame_pos = positions.reshape(FRAMES, FRAME_PILOTS)
    key_pil_all = lookup_per_round[frame_pos]
    val_pil_all = content_per_round[frame_pos]
    key_pad = jnp.pad(lookup_per_round, ((HALF_SPAN, HALF_SPAN), (0, 0)))
    val_pad = jnp.pad(content_per_round, ((HALF_SPAN, HALF_SPAN), (0, 0)))
    extended_frame_label = jnp.pad(symbol_frame_label, (HALF_SPAN, HALF_SPAN), constant_values=-1)
    neighborhood_breadth = PIECE_SYMBOLS + 2 * HALF_SPAN

    def shard_step(running, current_shard_index):
        keypad_grad, valpad_grad, keypil_sum, valpil_sum, weight_sum = running
        first_line = (current_shard_index * PIECE_SYMBOLS).astype(jnp.int32)
        frame_index = (current_shard_index // FRAME_SHARDS).astype(jnp.int32)
        query_block = lax.dynamic_slice_in_dim(asker_per_round, first_line, PIECE_SYMBOLS, 0)
        grad_block = lax.dynamic_slice_in_dim(derivative_per_round, first_line, PIECE_SYMBOLS, 0)
        att_block = lax.dynamic_slice_in_dim(grad_att, first_line, PIECE_SYMBOLS, 0)
        key_win = lax.dynamic_slice_in_dim(key_pad, first_line, neighborhood_breadth, 0)
        val_win = lax.dynamic_slice_in_dim(val_pad, first_line, neighborhood_breadth, 0)
        local_admit_filter = joint_admit_filter(lax.dynamic_slice_in_dim(extended_frame_label, first_line, neighborhood_breadth, 0), PIECE_SYMBOLS)
        key_pil = lax.dynamic_index_in_dim(key_pil_all, frame_index, 0, keepdims=False)
        val_pil = lax.dynamic_index_in_dim(val_pil_all, frame_index, 0, keepdims=False)
        results = attend_shard(query_block, key_win, val_win, key_pil, val_pil, local_admit_filter, att_block)
        attended, query_grad, keywin_grad, valwin_grad, keypil_grad, valpil_grad = results
        keywin_round = lax.optimization_barrier(keywin_grad.astype(jnp.bfloat16)).astype(jnp.float32)
        valwin_round = lax.optimization_barrier(valwin_grad.astype(jnp.bfloat16)).astype(jnp.float32)
        keypad_grad = lax.dynamic_update_slice_in_dim(keypad_grad, lax.dynamic_slice_in_dim(keypad_grad, first_line, neighborhood_breadth, 0) + keywin_round, first_line, 0)
        valpad_grad = lax.dynamic_update_slice_in_dim(valpad_grad, lax.dynamic_slice_in_dim(valpad_grad, first_line, neighborhood_breadth, 0) + valwin_round, first_line, 0)
        key_round = lax.optimization_barrier(keypil_grad.astype(jnp.bfloat16)).astype(jnp.float32)
        val_round = lax.optimization_barrier(valpil_grad.astype(jnp.bfloat16)).astype(jnp.float32)
        keypil_sum = lax.dynamic_update_index_in_dim(keypil_sum, lax.dynamic_index_in_dim(keypil_sum, frame_index, 0, keepdims=False) + key_round, frame_index, 0)
        valpil_sum = lax.dynamic_update_index_in_dim(valpil_sum, lax.dynamic_index_in_dim(valpil_sum, frame_index, 0, keepdims=False) + val_round, frame_index, 0)
        weight_sum = weight_sum + jnp.dot(attended.T, grad_block, preferred_element_type=jnp.float32)
        mixed_block = jnp.dot(attended, result_weight_matrix, preferred_element_type=jnp.float32).astype(jnp.bfloat16)
        return ((keypad_grad, valpad_grad, keypil_sum, valpil_sum, weight_sum), (mixed_block, query_grad.astype(jnp.bfloat16)))
    initial = (jnp.zeros((ROUND_SYMBOLS + 2 * HALF_SPAN, D), jnp.float32), jnp.zeros((ROUND_SYMBOLS + 2 * HALF_SPAN, D), jnp.float32), jnp.zeros((FRAMES, FRAME_PILOTS, D), jnp.float32), jnp.zeros((FRAMES, FRAME_PILOTS, D), jnp.float32), jnp.zeros((D, D), jnp.float32))
    running, blocks = lax.scan(shard_step, initial, jnp.arange(N_SEQ, dtype=jnp.int32))
    keypad_grad, valpad_grad, keypil_sum, valpil_sum, weight_sum = running
    mixed_blocks, qgrad_blocks = blocks
    flat_pos = frame_pos.reshape(-1)
    key_grad = keypad_grad[HALF_SPAN:HALF_SPAN + ROUND_SYMBOLS].at[flat_pos].add(keypil_sum.reshape(-1, D))
    value_grad = valpad_grad[HALF_SPAN:HALF_SPAN + ROUND_SYMBOLS].at[flat_pos].add(valpil_sum.reshape(-1, D))
    return (mixed_blocks.reshape(ROUND_SYMBOLS, D), qgrad_blocks.reshape(ROUND_SYMBOLS, D), key_grad.astype(jnp.bfloat16), value_grad.astype(jnp.bfloat16), weight_sum)

def reference(mapped_askers, mapped_lookups, mapped_contents, result_cotangent, result_weight_matrix, reference_comb_shift, symbol_frame_label):

    def pass_fn(round_arguments):
        return round_iteration(round_arguments[0], round_arguments[1], round_arguments[2], round_arguments[3], result_weight_matrix, reference_comb_shift, symbol_frame_label)
    mixed, query_grad, key_grad, value_grad, weight_parts = lax.map(pass_fn, (mapped_askers, mapped_lookups, mapped_contents, result_cotangent))
    weight_grad = lax.optimization_barrier(jnp.sum(weight_parts, axis=0)) / math.sqrt(PASSES * ROUND_SYMBOLS)
    return (mixed, query_grad, key_grad, value_grad, weight_grad)
```

```python
import functools
import math

import jax
import jax.numpy as jnp
from jax import lax
from jax.experimental import pallas as pl
from jax.experimental.pallas import tpu as pltpu
from jax.sharding import PartitionSpec as P

HEADS = 8
HALF_SPAN = 256
FRAME_SHARDS = 8
MESH = pl.DeviceIdType.MESH
F32 = jnp.float32
BF16 = jnp.bfloat16


def dot_nt(a, b):
    return lax.dot_general(a, b, (((1,), (1,)), ((), ())), preferred_element_type=F32)


def dot_tn(a, b):
    return lax.dot_general(a, b, (((0,), (0,)), ((), ())), preferred_element_type=F32)


def dot_nn(a, b):
    return lax.dot_general(a, b, (((1,), (0,)), ((), ())), preferred_element_type=F32)


def attention_kernel(
    frames,
    rows,
    head_dim,
    pil,
    k_ref,
    v_ref,
    q_ref,
    g_ref,
    p_ref,
    klab_ref,
    qlab_ref,
    att_ref,
    dq_ref,
    dk_ref,
    dv_ref,
    kb,
    vb,
    qb,
    gb,
    pb,
    kpil,
    vpil,
    dka,
    dva,
    dkp,
    dvp,
    att_st,
    dq_st,
    dk_st,
    dv_st,
    hg_out,
    hg_in,
    send_in,
    recv_in,
    loc_in,
    send_h,
    recv_h,
    send_hg,
    recv_hg,
    send_out,
    recv_out,
    loc_out,
):
    seq = lax.axis_index("seq")
    me = seq % FRAME_SHARDS
    frame = seq // FRAME_SHARDS
    base = frame * FRAME_SHARDS
    has_left = frame > 0
    has_right = frame < frames - 1
    scale = 1.0 / math.sqrt(head_dim)
    n = FRAME_SHARDS

    def cols(h):
        return pl.ds(pl.multiple_of(h * head_dim, head_dim), head_dim)

    def block(b):
        return pl.ds(pl.multiple_of(b * rows, rows), rows)

    barrier = pltpu.get_barrier_semaphore()

    def greet(t, carry):
        pl.semaphore_signal(
            barrier, inc=1, device_id={"seq": base + (me + t) % n}, device_id_type=MESH
        )
        return carry

    lax.fori_loop(1, n, greet, 0)

    @pl.when(has_left)
    def _():
        pl.semaphore_signal(barrier, inc=1, device_id={"seq": seq - n}, device_id_type=MESH)

    @pl.when(has_right)
    def _():
        pl.semaphore_signal(barrier, inc=1, device_id={"seq": seq + n}, device_id_type=MESH)

    sides = has_left.astype(jnp.int32) + has_right.astype(jnp.int32)
    pl.semaphore_wait(barrier, n - 1 + sides)

    def source(i, peer):
        if i == 0:
            return p_ref
        return (k_ref, v_ref, q_ref, g_ref)[i - 1].at[:, cols(peer)]

    def landing(i, src):
        if i == 0:
            return pb.at[src]
        if i <= 2:
            return (kb, vb)[i - 1].at[block(src + 1)]
        return (qb, gb)[i - 3].at[block(src)]

    def in_copy(i, peer, src):
        return pltpu.make_async_remote_copy(
            src_ref=source(i, peer),
            dst_ref=landing(i, src),
            send_sem=send_in.at[i, peer],
            recv_sem=recv_in.at[i, src],
            device_id={"seq": base + peer},
            device_id_type=MESH,
        )

    for i in range(5):

        def send_one(t, carry, i=i):
            in_copy(i, (me + t) % n, me).start()
            return carry

        lax.fori_loop(1, n, send_one, 0)
        pltpu.make_async_copy(source(i, me), landing(i, me), loc_in.at[i]).start()

    zero_halo = jnp.zeros((rows, head_dim), BF16)

    @pl.when(jnp.logical_not(has_left))
    def _():
        kb[0:rows] = zero_halo
        vb[0:rows] = zero_halo

    @pl.when(jnp.logical_not(has_right))
    def _():
        kb[(n + 1) * rows : (n + 2) * rows] = zero_halo
        vb[(n + 1) * rows : (n + 2) * rows] = zero_halo

    dka[...] = jnp.zeros_like(dka)
    dva[...] = jnp.zeros_like(dva)
    dkp[...] = jnp.zeros_like(dkp)
    dvp[...] = jnp.zeros_like(dvp)

    def wait_in(i):
        def wait_one(t, carry):
            in_copy(i, (me + t) % n, (me + t) % n).wait_recv()
            return carry

        lax.fori_loop(1, n, wait_one, 0)
        pltpu.make_async_copy(source(i, me), landing(i, me), loc_in.at[i]).wait()

    def halo_copy(i, to_right):
        buf = (kb, vb)[i]
        s = 2 * i + (0 if to_right else 1)
        return pltpu.make_async_remote_copy(
            src_ref=buf.at[pl.ds((n if to_right else 1) * rows, rows)],
            dst_ref=buf.at[pl.ds((0 if to_right else n + 1) * rows, rows)],
            send_sem=send_h.at[s],
            recv_sem=recv_h.at[s],
            device_id={"seq": seq + n if to_right else seq - n},
            device_id_type=MESH,
        )

    wait_in(0)
    for i in range(2):
        wait_in(1 + i)

        @pl.when(has_right)
        def _(i=i):
            halo_copy(i, True).start()

        @pl.when(has_left)
        def _(i=i):
            halo_copy(i, False).start()

        def pick(s, carry, i=i):
            picked = dot_nn(pb[s], (kb, vb)[i][block(s + 1), :])
            (kpil, vpil)[i][s] = picked.astype(BF16)
            return carry

        lax.fori_loop(0, n, pick, 0)
    wait_in(3)
    wait_in(4)

    for i in range(2):

        @pl.when(has_right)
        def _(i=i):
            halo_copy(i, True).wait_send()
            halo_copy(i, False).wait_recv()

        @pl.when(has_left)
        def _(i=i):
            halo_copy(i, False).wait_send()
            halo_copy(i, True).wait_recv()

    stages = (att_st, dq_st, dk_st, dv_st)
    outs = (att_ref, dq_ref, dk_ref, dv_ref)

    def out_copy(i, peer, col):
        return pltpu.make_async_remote_copy(
            src_ref=stages[i].at[peer],
            dst_ref=outs[i].at[:, cols(col)],
            send_sem=send_out.at[i, peer],
            recv_sem=recv_out.at[i, col],
            device_id={"seq": base + peer},
            device_id_type=MESH,
        )

    def own_copy(i):
        return pltpu.make_async_copy(stages[i].at[me], outs[i].at[:, cols(me)], loc_out.at[i])

    def ship(i, b):
        @pl.when(b != me)
        def _():
            out_copy(i, b, me).start()

        @pl.when(b == me)
        def _():
            own_copy(i).start()

    span = rows + 2 * HALF_SPAN
    key_at = lax.broadcasted_iota(jnp.int32, (span, rows), 0)
    query_at = lax.broadcasted_iota(jnp.int32, (span, rows), 1)
    near = (key_at >= query_at) & (key_at <= query_at + 2 * HALF_SPAN)
    to_exp2 = scale * math.log2(math.e)

    def query_block(t, carry):
        b = (me + 1 + t) % n
        wide = pl.ds(pl.multiple_of(b * rows, rows), span)
        q = qb[block(b), :]
        g = gb[block(b), :]
        kw = kb[wide, :]
        vw = vb[wide, :]
        kp = kpil[...].reshape(n * pil, head_dim)
        vp = vpil[...].reshape(n * pil, head_dim)
        mask = near & (klab_ref[wide, :] == qlab_ref[pl.ds(b, 1), :])
        s_w = jnp.where(mask, dot_nt(kw, q), -jnp.inf)
        s_p = dot_nt(kp, q)
        top = jnp.maximum(jnp.max(s_w, 0, keepdims=True), jnp.max(s_p, 0, keepdims=True))
        e_w = jnp.exp2((s_w - top) * to_exp2)
        e_p = jnp.exp2((s_p - top) * to_exp2)
        inv = 1.0 / (jnp.sum(e_w, 0, keepdims=True) + jnp.sum(e_p, 0, keepdims=True))
        p_w = e_w * inv
        p_p = e_p * inv
        w_w = p_w.astype(BF16)
        w_p = p_p.astype(BF16)
        att_t = (dot_tn(vw, w_w) + dot_tn(vp, w_p)).astype(BF16).astype(F32)
        att_st[b] = att_t.T.astype(BF16)
        ship(0, b)
        delta = jnp.sum(g.astype(F32).T * att_t, 0, keepdims=True)
        d_w = (p_w * (dot_nt(vw, g) - delta)).astype(BF16)
        d_p = (p_p * (dot_nt(vp, g) - delta)).astype(BF16)
        dq_t = (dot_tn(kw, d_w) + dot_tn(kp, d_p)) * scale
        dq_st[b] = dq_t.T.astype(BF16)
        ship(1, b)
        dva[wide, :] += dot_nn(w_w, g)
        dvp[...] += dot_nn(w_p, g)
        dka[wide, :] += dot_nn(d_w, q)
        dkp[...] += dot_nn(d_p, q)
        return carry

    lax.fori_loop(0, n, query_block, 0)

    def edge_copy(i, to_right):
        s = 2 * i + (0 if to_right else 1)
        return pltpu.make_async_remote_copy(
            src_ref=hg_out.at[s],
            dst_ref=hg_in.at[s],
            send_sem=send_hg.at[s],
            recv_sem=recv_hg.at[s],
            device_id={"seq": seq + n if to_right else seq - n},
            device_id_type=MESH,
        )

    factor = (scale, 1.0)
    sums = (dka, dva)
    pilot_sums = (dkp, dvp)
    for i in range(2):

        @pl.when(has_right)
        def _(i=i):
            hg_out[2 * i] = (sums[i][(n + 1) * rows : (n + 2) * rows, :] * factor[i]).astype(BF16)
            edge_copy(i, True).start()

        @pl.when(has_left)
        def _(i=i):
            hg_out[2 * i + 1] = (sums[i][0:rows, :] * factor[i]).astype(BF16)
            edge_copy(i, False).start()

    def finish(i, s):
        pilots = pilot_sums[i][pl.ds(pl.multiple_of(s * pil, pil), pil), :]
        high = pilots.astype(BF16)
        low = (pilots - high.astype(F32)).astype(BF16)
        places = pb[s]
        total = sums[i][block(s + 1), :] + (dot_tn(places, high) + dot_tn(places, low))
        return total * factor[i]

    def middle(t, carry):
        s = (me + 1 + t) % n

        @pl.when((s != 0) & (s != n - 1))
        def _():
            for i in range(2):
                stages[2 + i][s] = finish(i, s).astype(BF16)
                ship(2 + i, s)

        return carry

    lax.fori_loop(0, n, middle, 0)
    for i in range(2):

        @pl.when(has_left)
        def _(i=i):
            edge_copy(i, False).wait_send()
            edge_copy(i, True).wait_recv()
            stages[2 + i][0] = (finish(i, 0) + hg_in[2 * i].astype(F32)).astype(BF16)

        @pl.when(jnp.logical_not(has_left))
        def _(i=i):
            stages[2 + i][0] = finish(i, 0).astype(BF16)

        ship(2 + i, 0)

        @pl.when(has_right)
        def _(i=i):
            edge_copy(i, True).wait_send()
            edge_copy(i, False).wait_recv()
            stages[2 + i][n - 1] = (finish(i, n - 1) + hg_in[2 * i + 1].astype(F32)).astype(BF16)

        @pl.when(jnp.logical_not(has_right))
        def _(i=i):
            stages[2 + i][n - 1] = finish(i, n - 1).astype(BF16)

        ship(2 + i, n - 1)

    def drain(t, carry):
        peer = (me + t) % n
        for i in range(5):
            in_copy(i, peer, me).wait_send()
        for i in range(4):
            out_copy(i, peer, me).wait_send()
            out_copy(i, peer, peer).wait_recv()
        return carry

    lax.fori_loop(1, n, drain, 0)
    for i in range(4):
        own_copy(i).wait()


def attend(k, v, q, g, places, key_labels, query_labels, frames):
    rows, width = q.shape
    head_dim = width // HEADS
    pil = places.shape[0]
    n = FRAME_SHARDS
    out = jax.ShapeDtypeStruct((rows, width), BF16)
    hbm = pl.BlockSpec(memory_space=pl.ANY)
    vmem = pl.BlockSpec(memory_space=pltpu.VMEM)
    dma = pltpu.SemaphoreType.DMA
    return pl.pallas_call(
        functools.partial(attention_kernel, frames, rows, head_dim, pil),
        out_shape=(out,) * 4,
        in_specs=[hbm] * 5 + [vmem] * 2,
        out_specs=(hbm,) * 4,
        scratch_shapes=[
            pltpu.VMEM(((n + 2) * rows, head_dim), BF16),
            pltpu.VMEM(((n + 2) * rows, head_dim), BF16),
            pltpu.VMEM((n * rows, head_dim), BF16),
            pltpu.VMEM((n * rows, head_dim), BF16),
            pltpu.VMEM((n, pil, rows), BF16),
            pltpu.VMEM((n, pil, head_dim), BF16),
            pltpu.VMEM((n, pil, head_dim), BF16),
            pltpu.VMEM(((n + 2) * rows, head_dim), F32),
            pltpu.VMEM(((n + 2) * rows, head_dim), F32),
            pltpu.VMEM((n * pil, head_dim), F32),
            pltpu.VMEM((n * pil, head_dim), F32),
            pltpu.VMEM((n, rows, head_dim), BF16),
            pltpu.VMEM((n, rows, head_dim), BF16),
            pltpu.VMEM((n, rows, head_dim), BF16),
            pltpu.VMEM((n, rows, head_dim), BF16),
            pltpu.VMEM((4, rows, head_dim), BF16),
            pltpu.VMEM((4, rows, head_dim), BF16),
            dma((5, n)),
            dma((5, n)),
            dma((5,)),
            dma((4,)),
            dma((4,)),
            dma((4,)),
            dma((4,)),
            dma((4, n)),
            dma((4, n)),
            dma((4,)),
        ],
        compiler_params=pltpu.CompilerParams(
            collective_id=0, has_side_effects=True, vmem_limit_bytes=40 * 1024 * 1024
        ),
    )(k, v, q, g, places, key_labels, query_labels)


def on_device(
    mapped_askers,
    mapped_lookups,
    mapped_contents,
    result_cotangent,
    result_weight_matrix,
    reference_comb_shift,
    symbol_frame_label,
):
    grad_block = result_cotangent[0]
    rows = grad_block.shape[0]
    shards = lax.axis_size("seq")
    frames = shards // FRAME_SHARDS
    pil = reference_comb_shift.shape[1]
    frame = lax.axis_index("seq") // FRAME_SHARDS
    grad_att = jnp.dot(grad_block, result_weight_matrix.T, preferred_element_type=F32).astype(BF16)
    slots = jnp.arange(pil, dtype=jnp.int32) * (rows // pil) + reference_comb_shift[0]
    places = (slots[:, None] == jnp.arange(rows, dtype=jnp.int32)[None, :]).astype(BF16)
    extended = jnp.pad(symbol_frame_label, (HALF_SPAN, HALF_SPAN), constant_values=-1)
    tokens = FRAME_SHARDS * rows
    key_labels = lax.dynamic_slice_in_dim(extended, frame * tokens, tokens + 2 * HALF_SPAN, 0)
    query_labels = key_labels[HALF_SPAN : HALF_SPAN + tokens].reshape(FRAME_SHARDS, rows)
    attended, query_grad, key_grad, value_grad = attend(
        mapped_lookups[0],
        mapped_contents[0],
        mapped_askers[0],
        grad_att,
        places,
        key_labels[:, None],
        query_labels,
        frames,
    )
    mixed = jnp.dot(attended, result_weight_matrix, preferred_element_type=F32).astype(BF16)
    share = lax.dot_general(
        attended, grad_block, (((0,), (0,)), ((), ())), preferred_element_type=F32
    )
    total = lax.psum_scatter(share, ("dp", "seq"), scatter_dimension=0, tiled=True)
    weight_grad = total / math.sqrt(lax.axis_size("dp") * shards * rows)
    return (mixed[None], query_grad[None], key_grad[None], value_grad[None], weight_grad)


def solution(mesh):
    row_spec = P("dp", "seq", None)
    return jax.shard_map(
        on_device,
        mesh=mesh,
        in_specs=(row_spec, row_spec, row_spec, row_spec, P(), P("seq", None), P()),
        out_specs=(row_spec, row_spec, row_spec, row_spec, P(("dp", "seq"), None)),
        check_vma=False,
    )
```
